32 devices in a mesh: dp: 2 (over core), expert: 16 (over z, y, x).
Axes of the slice: x: 2, y: 2, z: 4, core: 2. Of those that a mesh axis runs over, the one named last changes fastest.
Arguments:
- tokens: bfloat16 [4096, 2048], P(('dp', 'expert')), may hold values from -6 to 6
- out_grad: bfloat16 [4096, 2048], P(('dp', 'expert')), may hold values from -3 to 3
- expert_ids: int32 [4096, 1], P(('dp', 'expert')), may hold values from 0 to 7, as said below
- gate_fixed: int32 [4096, 1], P(('dp', 'expert')), may hold values from 8192 to 65535
- w_gate: bfloat16 [16, 2048, 384], P('expert', 'dp'), may hold values from -0.125 to 0.125
- w_up: bfloat16 [16, 2048, 384], P('expert', 'dp'), may hold values from -0.125 to 0.125
- w_down: bfloat16 [16, 384, 2048], P('expert', None, 'dp'), may hold values from -0.21875 to 0.21875
- m_gate: float32 [16, 2048, 384], P('expert', 'dp'), may hold values from -12 to 12
- m_up: float32 [16, 2048, 384], P('expert', 'dp'), may hold values from -12 to 12
- m_down: float32 [16, 384, 2048], P('expert', None, 'dp'), may hold values from -12 to 12
- v_gate: float32 [16, 2048, 384], P('expert', 'dp'), may hold values from 1 to 100
- v_up: float32 [16, 2048, 384], P('expert', 'dp'), may hold values from 1 to 100
- v_down: float32 [16, 384, 2048], P('expert', None, 'dp'), may hold values from 1 to 100
Outputs:
- input_grad: bfloat16 [4096, 2048], P(('dp', 'expert'))
- new_w_gate: bfloat16 [16, 2048, 384], P('expert', 'dp')
- new_w_up: bfloat16 [16, 2048, 384], P('expert', 'dp')
- new_w_down: bfloat16 [16, 384, 2048], P('expert', None, 'dp')
- new_m_gate: float32 [16, 2048, 384], P('expert', 'dp')
- new_m_up: float32 [16, 2048, 384], P('expert', 'dp')
- new_m_down: float32 [16, 384, 2048], P('expert', None, 'dp')
- new_v_gate: float32 [16, 2048, 384], P('expert', 'dp')
- new_v_up: float32 [16, 2048, 384], P('expert', 'dp')
- new_v_down: float32 [16, 384, 2048], P('expert', None, 'dp')
The draws below stay inside these ranges and needn't reach their ends.
Inputs may be any that keep to these rules, and one draw needn't show every extreme that they name: `expert_ids`: in each aligned block of 128 tokens (the tokens of one device) one expert, the same in every block, is named exactly 32 times; every other expert is named at most 16 times, and some other expert exactly 16 times in every block.
All inputs are finite; a program needn't handle non-finite values.
Results may differ from the reference program's by a relative error of at most 0.024.
Values may be sent and summed in bfloat16 or wider, within the bound.
A program may use at most 128 MiB of HBM per device.

```python
import math
import jax
import jax.numpy as jnp
from jax import lax

D = 2048
FF = 768
TOK_DEV = 128
HALF = 384
EXPERTS = 8
CAP = 16
HOT = 32
TOKENS = 4096


def draw_expert_ids(key, part):
    blocks = TOKENS // TOK_DEV
    hot_key, rest_key = jax.random.split(jax.random.fold_in(key, 11))
    hottest = jax.random.randint(hot_key, (), 0, EXPERTS).astype(jnp.int32)

    def one_block(block_index):
        block_key = jax.random.fold_in(rest_key, block_index)
        second_key, pick_key, place_key = jax.random.split(block_key, 3)
        second = ((hottest + 1 + jax.random.randint(second_key, (), 0, EXPERTS - 1)) % EXPERTS).astype(jnp.int32)
        low_pick = jnp.minimum(hottest, second)
        high_pick = jnp.maximum(hottest, second)
        places = jax.random.permutation(pick_key, (EXPERTS - 2) * CAP)[:TOK_DEV - HOT - CAP]
        others = (places // CAP).astype(jnp.int32)
        others = others + (others >= low_pick).astype(jnp.int32)
        others = others + (others >= high_pick).astype(jnp.int32)
        labels = jnp.concatenate([jnp.full((HOT,), hottest, jnp.int32), jnp.full((CAP,), second, jnp.int32), others])
        shuffle = jax.random.permutation(place_key, TOK_DEV)
        return labels[shuffle]
    labels = jax.vmap(one_block)(jnp.arange(blocks, dtype=jnp.int32))
    return labels.reshape(TOKENS, 1).astype(jnp.int32)


def set_ends(values, rng, smallest, high):
    index_at = [jax.random.randint(jax.random.fold_in(rng, axis), (), 0, length) for axis, length in enumerate(values.shape)]
    widest = values.shape.index(max(values.shape))
    neighbour = index_at[:widest] + [(index_at[widest] + 1) % values.shape[widest]] + index_at[widest + 1:]
    return values.at[tuple(index_at)].set(smallest).at[tuple(neighbour)].set(high)


def level_of(key, shape, shards, least, largest):
    factor_of = 1.0
    for axis_at, parts in shards:
        heights = jax.random.uniform(jax.random.fold_in(jax.random.fold_in(key, 6), axis_at), (parts,), jnp.float32, least / len(shards), largest / len(shards))
        factor_of = factor_of * jnp.repeat(jnp.exp(heights), shape[axis_at] // parts).reshape((-1,) + (1,) * (len(shape) - 1 - axis_at))
    return factor_of


def normal_values(key, shape, deviation, reach, shards=(), kind=jnp.bfloat16):
    result = deviation * jax.random.normal(key, shape, jnp.float32)
    if shards:
        result = result * level_of(key, shape, shards, -0.22, 0.18)
    return jnp.clip(result, -reach, reach).astype(kind)


def setup_inputs(seed: int = 0) -> dict:
    key_of = jax.random.split(jax.random.key(seed), 14)
    return {
        "tokens": normal_values(key_of[0], (TOKENS, D), 1.0, 6.0, ((0, 32),)),
        "out_grad": normal_values(key_of[1], (TOKENS, D), 0.5, 3.0, ((0, 32),)),
        "expert_ids": draw_expert_ids(jax.random.fold_in(key_of[13], 71), 0),
        "gate_fixed": set_ends(jax.random.randint(key_of[3], (TOKENS, 1), 8192, 65536), jax.random.fold_in(key_of[3], 1), 8192, 65535).astype(jnp.int32),
        "w_gate": normal_values(key_of[4], (2 * EXPERTS, D, HALF), D ** -0.5, 0.125, ((0, 16), (1, 2))),
        "w_up": normal_values(key_of[5], (2 * EXPERTS, D, HALF), D ** -0.5, 0.125, ((0, 16), (1, 2))),
        "w_down": normal_values(key_of[6], (2 * EXPERTS, HALF, D), FF ** -0.5, 0.21875, ((0, 16), (2, 2))),
        "m_gate": normal_values(key_of[7], (2 * EXPERTS, D, HALF), 2.0, 12.0, ((0, 16), (1, 2)), jnp.float32),
        "m_up": normal_values(key_of[8], (2 * EXPERTS, D, HALF), 2.0, 12.0, ((0, 16), (1, 2)), jnp.float32),
        "m_down": normal_values(key_of[9], (2 * EXPERTS, HALF, D), 2.0, 12.0, ((0, 16), (2, 2)), jnp.float32),
        "v_gate": jnp.clip(jnp.exp(math.log(100.0) - 4.6051702 * jax.random.uniform(key_of[10], (2 * EXPERTS, D, HALF), jnp.float32) ** level_of(key_of[10], (2 * EXPERTS, D, HALF), ((0, 16), (1, 2)), -0.2, 0.2)), 1.0, 100.0),
        "v_up": jnp.clip(jnp.exp(math.log(100.0) - 4.6051702 * jax.random.uniform(key_of[11], (2 * EXPERTS, D, HALF), jnp.float32) ** level_of(key_of[11], (2 * EXPERTS, D, HALF), ((0, 16), (1, 2)), -0.2, 0.2)), 1.0, 100.0),
        "v_down": jnp.clip(jnp.exp(math.log(100.0) - 4.6051702 * jax.random.uniform(key_of[12], (2 * EXPERTS, HALF, D), jnp.float32) ** level_of(key_of[12], (2 * EXPERTS, HALF, D), ((0, 16), (2, 2)), -0.2, 0.2)), 1.0, 100.0),
    }


beta_one = 0.9
beta_two = 0.95
learn_rate = 0.002
decay_rate = 0.1
epsilon = 1e-08
bias_one = 1.0 - beta_one ** 20
bias_two = 1.0 - beta_two ** 20
fixed_scale = 1.0 / 65536.0
block_rows = 256

def expert_block(rows_input, rows_cotangent, gate_full, up_full, down_full):
    gate_pre = jnp.dot(rows_input, gate_full, preferred_element_type=jnp.float32)
    up_pre = jnp.dot(rows_input, up_full, preferred_element_type=jnp.float32)
    sigmoid_gate = jax.nn.sigmoid(gate_pre)
    active = gate_pre * sigmoid_gate
    hidden = (active * up_pre).astype(jnp.bfloat16)
    hidden_cot = jnp.dot(rows_cotangent, down_full.T, preferred_element_type=jnp.float32)
    grad_up = (hidden_cot * active).astype(jnp.bfloat16)
    grad_gate = (hidden_cot * up_pre * sigmoid_gate * (1.0 + gate_pre * (1.0 - sigmoid_gate))).astype(jnp.bfloat16)
    row_grad = jnp.dot(grad_gate, gate_full.T, preferred_element_type=jnp.float32) + jnp.dot(grad_up, up_full.T, preferred_element_type=jnp.float32)
    return (hidden, grad_gate, grad_up, row_grad)

def adam_update(weight, gradient, moment_one, moment_two):
    weight_full = weight.astype(jnp.float32)
    first_new = beta_one * moment_one + (1.0 - beta_one) * gradient
    second_new = beta_two * moment_two + (1.0 - beta_two) * gradient * gradient
    update = first_new / bias_one / (jnp.sqrt(second_new / bias_two) + epsilon) + decay_rate * weight_full
    return ((weight_full - learn_rate * update).astype(jnp.bfloat16), first_new, second_new)

def pair_join(array, expert, axis_index):
    pair_rows = lax.dynamic_slice_in_dim(array, 2 * expert, 2, 0)
    return jnp.concatenate([pair_rows[0], pair_rows[1]], axis=axis_index)

def pair_split(array, axis_index):
    halves = jnp.split(array, 2, axis=axis_index)
    return jnp.stack(halves)

def reference(tokens, out_grad, expert_ids, gate_fixed, w_gate, w_up, w_down, m_gate, m_up, m_down, v_gate, v_up, v_down):
    token_scale = gate_fixed[:, 0].astype(jnp.float32) * fixed_scale
    cotangent = (out_grad.astype(jnp.float32) * token_scale[:, None]).astype(jnp.bfloat16)
    chosen = expert_ids[:, 0].astype(jnp.int32)
    sorted_rows = jnp.argsort(chosen, stable=True).astype(jnp.int32)
    counts = jax.ops.segment_sum(jnp.ones((TOKENS,), jnp.int32), chosen, num_segments=EXPERTS).astype(jnp.int32)
    starts = (jnp.cumsum(counts) - counts).astype(jnp.int32)
    sorted_pad = jnp.concatenate([sorted_rows, jnp.full((block_rows,), TOKENS, jnp.int32)])
    input_pad = jnp.concatenate([tokens, jnp.zeros((1, D), tokens.dtype)], axis=0)
    cotangent_pad = jnp.concatenate([cotangent, jnp.zeros((1, D), cotangent.dtype)], axis=0)

    def per_expert(grad_rows, expert):
        gate_full = pair_join(w_gate, expert, 1)
        up_full = pair_join(w_up, expert, 1)
        down_full = pair_join(w_down, expert, 0)
        first_row = starts[expert]
        row_count = counts[expert]
        block_count = ((row_count + block_rows - 1) // block_rows).astype(jnp.int32)

        def per_block(block_index, block_state):
            grad_rows, gate_part, up_part, down_part = block_state
            positions = (first_row + block_index * block_rows + jnp.arange(block_rows, dtype=jnp.int32)).astype(jnp.int32)
            in_group = positions < first_row + row_count
            row_index = jnp.where(in_group, jnp.take(sorted_pad, positions), TOKENS).astype(jnp.int32)
            rows_input = jnp.take(input_pad, row_index, axis=0)
            rows_cotangent = jnp.take(cotangent_pad, row_index, axis=0)
            hidden, grad_gate, grad_up, row_grad = expert_block(rows_input, rows_cotangent, gate_full, up_full, down_full)
            gate_part = gate_part + jnp.dot(rows_input.T, grad_gate, preferred_element_type=jnp.float32)
            up_part = up_part + jnp.dot(rows_input.T, grad_up, preferred_element_type=jnp.float32)
            down_part = down_part + jnp.dot(hidden.T, rows_cotangent, preferred_element_type=jnp.float32)
            grad_rows = grad_rows.at[row_index].set(row_grad.astype(jnp.bfloat16))
            return (grad_rows, gate_part, up_part, down_part)
        zero_in = jnp.zeros((D, FF), jnp.float32)
        zero_out = jnp.zeros((FF, D), jnp.float32)
        grad_rows, gate_total, up_total, down_total = lax.fori_loop(jnp.int32(0), block_count, per_block, (grad_rows, zero_in, zero_in, zero_out))
        gate_new, gate_first, gate_second = adam_update(gate_full, gate_total, pair_join(m_gate, expert, 1), pair_join(v_gate, expert, 1))
        up_new, up_first, up_second = adam_update(up_full, up_total, pair_join(m_up, expert, 1), pair_join(v_up, expert, 1))
        down_new, down_first, down_second = adam_update(down_full, down_total, pair_join(m_down, expert, 0), pair_join(v_down, expert, 0))
        results = (pair_split(gate_new, 1), pair_split(up_new, 1), pair_split(down_new, 0), pair_split(gate_first, 1), pair_split(up_first, 1), pair_split(down_first, 0), pair_split(gate_second, 1), pair_split(up_second, 1), pair_split(down_second, 0))
        return (grad_rows, results)
    grad_init = jnp.zeros((TOKENS + 1, D), jnp.bfloat16)
    grad_rows, stacked = lax.scan(per_expert, grad_init, jnp.arange(EXPERTS, dtype=jnp.int32))
    flat = [jnp.reshape(item, (2 * EXPERTS,) + item.shape[2:]) for item in stacked]
    return (grad_rows[:TOKENS], flat[0], flat[1], flat[2], flat[3], flat[4], flat[5], flat[6], flat[7], flat[8])
```

```python
import functools

import jax
import jax.numpy as jnp
from jax import lax
from jax.experimental import pallas as pl
from jax.experimental.pallas import tpu as pltpu
from jax.sharding import PartitionSpec as P

beta_one = 0.9
beta_two = 0.95
learn_rate = 0.002
decay_rate = 0.1
epsilon = 1e-08
bias_one = 1.0 - beta_one**20
bias_two = 1.0 - beta_two**20
fixed_scale = 1.0 / 65536.0

f32 = jnp.float32
bf16 = jnp.bfloat16
MESH = pl.DeviceIdType.MESH
lhs_t = (((0,), (0,)), ((), ()))
rhs_t = (((1,), (1,)), ((), ()))


def adam_update(weight, gradient, moment_one, moment_two):
    weight_full = weight.astype(f32)
    first_new = beta_one * moment_one + (1.0 - beta_one) * gradient
    second_new = beta_two * moment_two + (1.0 - beta_two) * gradient * gradient
    update = (
        first_new / bias_one / (jnp.sqrt(second_new / bias_two) + epsilon)
        + decay_rate * weight_full
    )
    return ((weight_full - learn_rate * update).astype(bf16), first_new, second_new)


def flipped(index, mask, count):
    total, bit = 0, 1
    while bit < count:
        here = lax.rem(lax.div(index, bit), 2)
        total = total + (1 - here if mask & bit else here) * bit
        bit *= 2
    return total


def remote(src, dst, send, recv, where):
    return pltpu.make_async_remote_copy(
        src_ref=src, dst_ref=dst, send_sem=send, recv_sem=recv, device_id=where, device_id_type=MESH
    )


def kernel(
    n, experts, hot, bs,
    tok_ref, og_ref, ids_ref, fix_ref, wg_ref, wu_ref, wd_ref,
    grad_ref, gate_out, up_out, down_out,
    slots, rows, gu, dn, part, psend, precv, rsend, ret, inner, hid, gu_grad, dn_grad,
    gu_recv, dn_recv, pick,
    wl, ws, wr, d_send, d_recv, f_send, f_recv, p_send, p_recv, r_send, r_recv, g_send, g_recv,
):
    tok_rows, depth = tok_ref.shape
    ff = wg_ref.shape[2]
    dpart = depth // n
    nb = dpart // bs
    all_rows = experts * hot
    d = lax.axis_index("dp")
    g = lax.axis_index("expert")
    e = lax.div(g, 2)
    s = lax.rem(g, 2)
    partner = g + 1 - 2 * s
    near, far = range(experts // 2), range(experts // 2, experts)
    order = [k for pair in zip(near, far) for k in pair]

    def peer(k):
        return {"expert": 2 * flipped(e, k, experts) + s}

    def dp_at(k):
        return lax.rem(d + k, n)

    def places(owner):
        at = pl.ds(pl.multiple_of(owner * dpart, dpart), dpart)
        return [gu.at[at, pl.ds(0, ff)], gu.at[at, pl.ds(ff, ff)], dn.at[:, at]]

    weights = [wg_ref.at[0], wu_ref.at[0], wd_ref.at[0]]
    local = [pltpu.make_async_copy(w, to, wl.at[i]) for i, (w, to) in enumerate(zip(weights, places(d)))]
    for copy in local:
        copy.start()

    barrier = pltpu.get_barrier_semaphore()
    for k in range(1, experts):
        pl.semaphore_signal(barrier, inc=1, device_id=peer(k), device_id_type=MESH)
    pl.semaphore_signal(barrier, inc=1, device_id={"expert": partner}, device_id_type=MESH)
    for k in range(1, n):
        pl.semaphore_signal(barrier, inc=1, device_id={"dp": dp_at(k)}, device_id_type=MESH)

    ids = ids_ref[...]
    chosen = ids == lax.broadcasted_iota(jnp.int32, (tok_rows, experts), 1)
    onehot = chosen.astype(f32)
    before = lax.broadcasted_iota(jnp.int32, (tok_rows, tok_rows), 1) < lax.broadcasted_iota(
        jnp.int32, (tok_rows, tok_rows), 0
    )
    counts = jnp.dot(before.astype(f32).astype(bf16), onehot.astype(bf16), preferred_element_type=f32)
    position = jnp.sum(counts * onehot, axis=1, keepdims=True)
    slot = ids.astype(f32) * hot + position
    lanes = lax.broadcasted_iota(jnp.int32, (tok_rows, all_rows), 1).astype(f32)
    chosen_slot = jnp.where(slot == lanes, 1.0, 0.0).astype(f32)
    pick[...] = chosen_slot.astype(bf16)
    scale = fix_ref[...].astype(f32) * fixed_scale
    cot = (og_ref[...].astype(f32) * scale).astype(bf16)
    for a, source in ((0, tok_ref[...]), (1, cot)):
        moved = lax.dot_general(pick[...], source, lhs_t, preferred_element_type=f32)
        slots[a] = moved.astype(bf16).reshape(experts, hot, depth)

    pl.semaphore_wait(barrier, experts + n - 1)

    sends = []

    def go(copy):
        copy.start()
        sends.append(copy)

    for pos, k in enumerate(order):
        for a in range(2):
            if k == 0:
                rows[a, 0, pos] = slots[a, e]
                go(remote(rows.at[a, 0, pos], rows.at[a, 1, pos], f_send.at[a, pos], f_recv.at[a, pos],
                          {"expert": partner}))
            else:
                go(remote(slots.at[a, flipped(e, k, experts)], rows.at[a, 0, pos], d_send.at[a, pos],
                          d_recv.at[a, pos], peer(k)))
    for k in range(1, n):
        for i in range(3):
            go(remote(weights[i], places(d)[i], ws.at[k - 1, i], wr.at[k - 1, i], {"dp": dp_at(k)}))

    for pos, k in enumerate(order):
        if k == 0:
            continue
        for a in range(2):
            remote(rows.at[a, 0, pos], rows.at[a, 0, pos], d_send.at[a, pos], d_recv.at[a, pos],
                   peer(k)).wait_recv()
            go(remote(rows.at[a, 0, pos], rows.at[a, 1, pos], f_send.at[a, pos], f_recv.at[a, pos],
                      {"expert": partner}))

    for copy in local:
        copy.wait()
    for k in range(1, n):
        arriving = places(lax.rem(d + n - k, n))
        for i in range(3):
            remote(arriving[i], arriving[i], ws.at[k - 1, i], wr.at[k - 1, i], {"dp": dp_at(k)}).wait_recv()

    def through(b, lo, many):
        here = pl.ds(lo, many)
        x = rows[0, b, here].reshape(many * hot, depth)
        c = rows[1, b, here].reshape(many * hot, depth)
        pre = jnp.dot(x, gu[...], preferred_element_type=f32)
        hidden_cot = lax.dot_general(c, dn[...], rhs_t, preferred_element_type=f32)
        gate_pre, up_pre = pre[:, :ff], pre[:, ff:]
        sig = jax.nn.sigmoid(gate_pre)
        active = gate_pre * sig
        at = pl.ds(b * all_rows + lo * hot, many * hot)
        hid[at] = (active * up_pre).astype(bf16)
        inner[at, pl.ds(ff, ff)] = (hidden_cot * active).astype(bf16)
        inner[at, pl.ds(0, ff)] = (hidden_cot * up_pre * sig * (1.0 + gate_pre * (1.0 - sig))).astype(bf16)
        return lax.dot_general(inner[at], gu[...], rhs_t, preferred_element_type=f32).reshape(many, hot, depth)

    part[...] = through(0, 0, experts)
    half = experts // 2
    for lo in (0, half):
        for pos in range(lo, lo + half):
            for a in range(2):
                remote(rows.at[a, 1, pos], rows.at[a, 1, pos], f_send.at[a, pos], f_recv.at[a, pos],
                       {"expert": partner}).wait_recv()
        psend[pl.ds(lo, half)] = through(1, lo, half).astype(bf16)
        for pos in range(lo, lo + half):
            go(remote(psend.at[pos], precv.at[pos], p_send.at[pos], p_recv.at[pos], {"expert": partner}))

    def weight_block(i, carry):
        block = lax.rem((d + 1) * nb + i, n * nb)
        at = pl.ds(pl.multiple_of(block * bs, bs), bs)
        x = rows[0, :, :, :, at].reshape(2 * all_rows, bs)
        c = rows[1, :, :, :, at].reshape(2 * all_rows, bs)
        gu_grad[block] = lax.dot_general(x, inner[...], lhs_t, preferred_element_type=f32)
        dn_grad[block] = lax.dot_general(hid[...], c, lhs_t, preferred_element_type=f32)
        return carry

    lax.fori_loop(0, (n - 1) * nb, weight_block, 0)
    for k in range(1, n):
        theirs = pl.ds(dp_at(k) * nb, nb)
        go(remote(gu_grad.at[theirs], gu_recv.at[k - 1], g_send.at[k - 1, 0], g_recv.at[k - 1, 0], {"dp": dp_at(k)}))
        go(remote(dn_grad.at[theirs], dn_recv.at[k - 1], g_send.at[k - 1, 1], g_recv.at[k - 1, 1], {"dp": dp_at(k)}))

    def give_back(pos):
        k = order[pos]
        remote(precv.at[pos], precv.at[pos], p_send.at[pos], p_recv.at[pos], {"expert": partner}).wait_recv()
        total = (part[pos] + precv[pos].astype(f32)).astype(bf16)
        if k == 0:
            ret[e] = total
        else:
            rsend[pos] = total
            go(remote(rsend.at[pos], ret.at[e], r_send.at[pos], r_recv.at[pos], peer(k)))

    for pos in range(half):
        give_back(pos)
    lax.fori_loop((n - 1) * nb, n * nb, weight_block, 0)
    for pos in range(half, experts):
        give_back(pos)

    for k in range(1, n):
        remote(gu_recv.at[k - 1], gu_recv.at[k - 1], g_send.at[k - 1, 0], g_recv.at[k - 1, 0],
               {"dp": dp_at(k)}).wait_recv()
        remote(dn_recv.at[k - 1], dn_recv.at[k - 1], g_send.at[k - 1, 1], g_recv.at[k - 1, 1],
               {"dp": dp_at(k)}).wait_recv()
    for i in range(nb):
        at = pl.ds(i * bs, bs)
        both = gu_grad[d * nb + i]
        down = dn_grad[d * nb + i]
        for k in range(1, n):
            both = both + gu_recv[k - 1, i]
            down = down + dn_recv[k - 1, i]
        gate_out[at] = both[:, :ff]
        up_out[at] = both[:, ff:]
        down_out[:, at] = down

    for pos, k in enumerate(order):
        if k:
            at = ret.at[flipped(e, k, experts)]
            remote(at, at, r_send.at[pos], r_recv.at[pos], peer(k)).wait_recv()
    back = ret[...].reshape(all_rows, depth)
    grad_ref[...] = jnp.dot(pick[...], back, preferred_element_type=f32).astype(bf16)
    for copy in sends:
        copy.wait_send()


def expert_layer(n, groups, tokens, out_grad, expert_ids, gate_fixed, w_gate, w_up, w_down):
    tok_rows, depth = tokens.shape
    ff = w_gate.shape[2]
    experts = groups // 2
    hot = tok_rows // 4
    dpart = depth // n
    bs = min(dpart, 512)
    nb = dpart // bs
    all_rows = experts * hot
    vmem = pl.BlockSpec(memory_space=pltpu.VMEM)
    hbm = pl.BlockSpec(memory_space=pl.ANY)
    dma = pltpu.SemaphoreType.DMA
    chunk = (experts, hot, depth)
    return pl.pallas_call(
        functools.partial(kernel, n, experts, hot, bs),
        out_shape=(
            jax.ShapeDtypeStruct((tok_rows, depth), bf16),
            jax.ShapeDtypeStruct((dpart, ff), f32),
            jax.ShapeDtypeStruct((dpart, ff), f32),
            jax.ShapeDtypeStruct((ff, dpart), f32),
        ),
        in_specs=[vmem] * 4 + [hbm] * 3,
        out_specs=(vmem,) * 4,
        scratch_shapes=[
            pltpu.VMEM((2,) + chunk, bf16),
            pltpu.VMEM((2, 2) + chunk, bf16),
            pltpu.VMEM((depth, 2 * ff), bf16),
            pltpu.VMEM((ff, depth), bf16),
            pltpu.VMEM(chunk, f32),
            pltpu.VMEM(chunk, bf16),
            pltpu.VMEM(chunk, bf16),
            pltpu.VMEM(chunk, bf16),
            pltpu.VMEM(chunk, bf16),
            pltpu.VMEM((2 * all_rows, 2 * ff), bf16),
            pltpu.VMEM((2 * all_rows, ff), bf16),
            pltpu.VMEM((n * nb, bs, 2 * ff), f32),
            pltpu.VMEM((n * nb, ff, bs), f32),
            pltpu.VMEM((n - 1, nb, bs, 2 * ff), f32),
            pltpu.VMEM((n - 1, nb, ff, bs), f32),
            pltpu.VMEM((tok_rows, all_rows), bf16),
            dma((3,)),
            dma((n - 1, 3)),
            dma((n - 1, 3)),
            dma((2, experts)),
            dma((2, experts)),
            dma((2, experts)),
            dma((2, experts)),
            dma((experts,)),
            dma((experts,)),
            dma((experts,)),
            dma((experts,)),
            dma((n - 1, 2)),
            dma((n - 1, 2)),
        ],
        compiler_params=pltpu.CompilerParams(
            collective_id=0, has_side_effects=True, vmem_limit_bytes=60 * 1024 * 1024
        ),
        name="expert_layer",
    )(tokens, out_grad, expert_ids, gate_fixed, w_gate, w_up, w_down)


def per_device(
    tokens,
    out_grad,
    expert_ids,
    gate_fixed,
    w_gate,
    w_up,
    w_down,
    m_gate,
    m_up,
    m_down,
    v_gate,
    v_up,
    v_down,
):
    n = lax.axis_size("dp")
    groups = lax.axis_size("expert")
    input_grad, gate_grad, up_grad, down_grad = expert_layer(
        n, groups, tokens, out_grad, expert_ids, gate_fixed, w_gate, w_up, w_down
    )
    gate_new, gate_first, gate_second = adam_update(w_gate[0], gate_grad, m_gate[0], v_gate[0])
    up_new, up_first, up_second = adam_update(w_up[0], up_grad, m_up[0], v_up[0])
    down_new, down_first, down_second = adam_update(w_down[0], down_grad, m_down[0], v_down[0])
    return (
        input_grad,
        gate_new[None],
        up_new[None],
        down_new[None],
        gate_first[None],
        up_first[None],
        down_first[None],
        gate_second[None],
        up_second[None],
        down_second[None],
    )


def solution(mesh):
    return jax.shard_map(
        per_device,
        mesh=mesh,
        in_specs=(
            P(("dp", "expert"), None),
            P(("dp", "expert"), None),
            P(("dp", "expert"), None),
            P(("dp", "expert"), None),
            P("expert", "dp", None),
            P("expert", "dp", None),
            P("expert", None, "dp"),
            P("expert", "dp", None),
            P("expert", "dp", None),
            P("expert", None, "dp"),
            P("expert", "dp", None),
            P("expert", "dp", None),
            P("expert", None, "dp"),
        ),
        out_specs=(
            P(("dp", "expert"), None),
            P("expert", "dp", None),
            P("expert", "dp", None),
            P("expert", None, "dp"),
            P("expert", "dp", None),
            P("expert", "dp", None),
            P("expert", None, "dp"),
            P("expert", "dp", None),
            P("expert", "dp", None),
            P("expert", None, "dp"),
        ),
        check_vma=False,
    )
```

```python
import functools
import math

import jax
import jax.numpy as jnp
from jax import lax
from jax.experimental import pallas as pl
from jax.experimental.pallas import tpu as pltpu
from jax.sharding import PartitionSpec as P

beta_one = 0.9
beta_two = 0.95
learn_rate = 0.002
decay_rate = 0.1
epsilon = 1e-08
bias_one = 1.0 - beta_one**20
bias_two = 1.0 - beta_two**20
fixed_scale = 1.0 / 65536.0

f32 = jnp.float32
bf16 = jnp.bfloat16
spare_bytes = 6 * 1024 * 1024
MESH = pl.DeviceIdType.MESH
lhs_t = (((0,), (0,)), ((), ()))
rhs_t = (((1,), (1,)), ((), ()))


def adam_update(weight, gradient, moment_one, moment_two):
    weight_full = weight.astype(f32)
    first_new = beta_one * moment_one + (1.0 - beta_one) * gradient
    second_new = beta_two * moment_two + (1.0 - beta_two) * gradient * gradient
    update = (
        first_new / bias_one / (jnp.sqrt(second_new / bias_two) + epsilon)
        + decay_rate * weight_full
    )
    return ((weight_full - learn_rate * update).astype(bf16), first_new, second_new)


def flipped(index, mask, count):
    total, bit = 0, 1
    while bit < count:
        here = lax.rem(lax.div(index, bit), 2)
        total = total + (1 - here if mask & bit else here) * bit
        bit *= 2
    return total


def remote(src, dst, send, recv, where):
    return pltpu.make_async_remote_copy(
        src_ref=src, dst_ref=dst, send_sem=send, recv_sem=recv, device_id=where, device_id_type=MESH
    )


def kernel(
    n, experts, hot, bs,
    tok_ref, og_ref, ids_ref, fix_ref, wg_ref, wu_ref, wd_ref,
    grad_ref, gate_out, up_out, down_out,
    slots, rows, gu, dn, part, psend, precv, rsend, ret, inner, hid, gu_grad, dn_grad,
    gu_recv, dn_recv, pick,
    wl, ws, wr, d_send, d_recv, f_send, f_recv, p_send, p_recv, r_send, r_recv, g_send, g_recv,
):
    tok_rows, depth = tok_ref.shape
    ff = wg_ref.shape[2]
    dpart = depth // n
    nb = dpart // bs
    all_rows = experts * hot
    d = lax.axis_index("dp")
    g = lax.axis_index("expert")
    e = lax.div(g, 2)
    s = lax.rem(g, 2)
    partner = g + 1 - 2 * s
    order = list(range(experts))
    half = experts // 2
    window = 3

    def peer(k):
        return {"expert": 2 * flipped(e, k, experts) + s}

    def dp_at(k):
        return lax.rem(d + k, n)

    def places(owner):
        at = pl.ds(pl.multiple_of(owner * dpart, dpart), dpart)
        return [gu.at[at, pl.ds(0, ff)], gu.at[at, pl.ds(ff, ff)], dn.at[:, at]]

    weights = [wg_ref.at[0], wu_ref.at[0], wd_ref.at[0]]
    local = [pltpu.make_async_copy(w, to, wl.at[i]) for i, (w, to) in enumerate(zip(weights, places(d)))]
    for copy in local:
        copy.start()

    barrier = pltpu.get_barrier_semaphore()
    for k in range(1, experts):
        pl.semaphore_signal(barrier, inc=1, device_id=peer(k), device_id_type=MESH)
    pl.semaphore_signal(barrier, inc=1, device_id={"expert": partner}, device_id_type=MESH)
    for k in range(1, n):
        pl.semaphore_signal(barrier, inc=1, device_id={"dp": dp_at(k)}, device_id_type=MESH)

    ids = ids_ref[...]
    onehot = (ids == lax.broadcasted_iota(jnp.int32, (experts, tok_rows), 0)).astype(f32)
    row_at = lax.broadcasted_iota(jnp.int32, (tok_rows, tok_rows), 0)
    col_at = lax.broadcasted_iota(jnp.int32, (tok_rows, tok_rows), 1)
    before = jnp.where(row_at < col_at, 1.0, 0.0).astype(bf16)
    counts = jnp.dot(onehot.astype(bf16), before, preferred_element_type=f32)
    position = jnp.sum(counts * onehot, axis=0, keepdims=True)
    slot = ids.astype(f32) * hot + position
    heights = lax.broadcasted_iota(jnp.int32, (all_rows, tok_rows), 0).astype(f32)
    pick[...] = jnp.where(slot == heights, 1.0, 0.0).astype(bf16)
    scale_row = fix_ref[...].astype(f32) * fixed_scale
    scale = jnp.sum(jnp.where(row_at == col_at, scale_row, 0.0), axis=1, keepdims=True)
    cot = (og_ref[...].astype(f32) * scale).astype(bf16)
    for a, source in ((0, tok_ref[...]), (1, cot)):
        moved = jnp.dot(pick[...], source, preferred_element_type=f32)
        slots[a] = moved.astype(bf16).reshape(experts, hot, depth)

    pl.semaphore_wait(barrier, experts + n - 1)

    sends = []

    def go(copy):
        copy.start()
        sends.append(copy)

    def forward(a, pos):
        go(remote(rows.at[a, 0, pos], rows.at[a, 1, pos], f_send.at[a, pos], f_recv.at[a, pos],
                  {"expert": partner}))

    def direct(a, pos):
        k = order[pos]
        go(remote(slots.at[a, flipped(e, k, experts)], rows.at[a, 0, pos], d_send.at[a, pos],
                  d_recv.at[a, pos], peer(k)))

    waiting = [(a, pos) for pos in range(half, experts) for a in range(2)]
    for a, pos in waiting[:window]:
        direct(a, pos)
    for pos in range(1, half):
        for a in range(2):
            direct(a, pos)
    for a in range(2):
        rows[a, 0, 0] = slots[a, e]
        forward(a, 0)
    for k in range(1, n):
        for i in range(3):
            go(remote(weights[i], places(d)[i], ws.at[k - 1, i], wr.at[k - 1, i], {"dp": dp_at(k)}))

    started = window
    for pos in range(1, experts):
        for a in range(2):
            remote(rows.at[a, 0, pos], rows.at[a, 0, pos], d_send.at[a, pos], d_recv.at[a, pos],
                   peer(order[pos])).wait_recv()
            if pos >= half and started < len(waiting):
                direct(*waiting[started])
                started += 1
            forward(a, pos)

    for copy in local:
        copy.wait()
    for k in range(1, n):
        arriving = places(lax.rem(d + n - k, n))
        for i in range(3):
            remote(arriving[i], arriving[i], ws.at[k - 1, i], wr.at[k - 1, i], {"dp": dp_at(k)}).wait_recv()

    def through(b, lo, many):
        here = pl.ds(lo, many)
        x = rows[0, b, here].reshape(many * hot, depth)
        c = rows[1, b, here].reshape(many * hot, depth)
        pre = jnp.dot(x, gu[...], preferred_element_type=f32)
        hidden_cot = lax.dot_general(c, dn[...], rhs_t, preferred_element_type=f32)
        gate_pre, up_pre = pre[:, :ff], pre[:, ff:]
        sig = jax.nn.sigmoid(gate_pre)
        active = gate_pre * sig
        at = pl.ds(b * all_rows + lo * hot, many * hot)
        hid[at] = (active * up_pre).astype(bf16)
        inner[at, pl.ds(ff, ff)] = (hidden_cot * active).astype(bf16)
        inner[at, pl.ds(0, ff)] = (hidden_cot * up_pre * sig * (1.0 + gate_pre * (1.0 - sig))).astype(bf16)
        return lax.dot_general(inner[at], gu[...], rhs_t, preferred_element_type=f32).reshape(many, hot, depth)

    for lo in (0, half):
        for pos in range(lo, lo + half):
            for a in range(2):
                remote(rows.at[a, 1, pos], rows.at[a, 1, pos], f_send.at[a, pos], f_recv.at[a, pos],
                       {"expert": partner}).wait_recv()
        psend[pl.ds(lo, half)] = through(1, lo, half).astype(bf16)
        for pos in range(lo, lo + half):
            go(remote(psend.at[pos], precv.at[pos], p_send.at[pos], p_recv.at[pos], {"expert": partner}))

    part[...] = through(0, 0, experts)

    def weight_block(i):
        block = lax.rem((d + 1) * nb + i, n * nb)
        at = pl.ds(pl.multiple_of(block * bs, bs), bs)
        x = rows[0, :, :, :, at].reshape(2 * all_rows, bs)
        c = rows[1, :, :, :, at].reshape(2 * all_rows, bs)
        gu_grad[block] = lax.dot_general(x, inner[...], lhs_t, preferred_element_type=f32)
        dn_grad[block] = lax.dot_general(hid[...], c, lhs_t, preferred_element_type=f32)
        if i % nb == nb - 1 and i < (n - 1) * nb:
            k = i // nb + 1
            theirs = pl.ds(dp_at(k) * nb, nb)
            go(remote(gu_grad.at[theirs], gu_recv.at[k - 1], g_send.at[k - 1, 0], g_recv.at[k - 1, 0],
                      {"dp": dp_at(k)}))
            go(remote(dn_grad.at[theirs], dn_recv.at[k - 1], g_send.at[k - 1, 1], g_recv.at[k - 1, 1],
                      {"dp": dp_at(k)}))

    def give_back(pos):
        k = order[pos]
        remote(precv.at[pos], precv.at[pos], p_send.at[pos], p_recv.at[pos], {"expert": partner}).wait_recv()
        total = (part[pos] + precv[pos].astype(f32)).astype(bf16)
        if k == 0:
            ret[e] = total
        else:
            rsend[pos] = total
            go(remote(rsend.at[pos], ret.at[e], r_send.at[pos], r_recv.at[pos], peer(k)))

    blocks = list(range(n * nb))
    for pos in range(experts):
        give_back(pos)
        if pos and blocks:
            weight_block(blocks.pop(0))
    for i in blocks:
        weight_block(i)

    for k in range(1, n):
        remote(gu_recv.at[k - 1], gu_recv.at[k - 1], g_send.at[k - 1, 0], g_recv.at[k - 1, 0],
               {"dp": dp_at(k)}).wait_recv()
        remote(dn_recv.at[k - 1], dn_recv.at[k - 1], g_send.at[k - 1, 1], g_recv.at[k - 1, 1],
               {"dp": dp_at(k)}).wait_recv()
    for i in range(nb):
        at = pl.ds(i * bs, bs)
        both = gu_grad[d * nb + i]
        down = dn_grad[d * nb + i]
        for k in range(1, n):
            both = both + gu_recv[k - 1, i]
            down = down + dn_recv[k - 1, i]
        gate_out[at] = both[:, :ff]
        up_out[at] = both[:, ff:]
        down_out[:, at] = down

    for pos, k in enumerate(order):
        if k:
            at = ret.at[flipped(e, k, experts)]
            remote(at, at, r_send.at[pos], r_recv.at[pos], peer(k)).wait_recv()
    back = ret[...].reshape(all_rows, depth)
    grad_ref[...] = lax.dot_general(pick[...], back, lhs_t, preferred_element_type=f32).astype(bf16)
    for copy in sends:
        copy.wait_send()


def expert_layer(n, groups, tokens, out_grad, expert_ids, gate_fixed, w_gate, w_up, w_down):
    tok_rows, depth = tokens.shape
    ff = w_gate.shape[2]
    experts = groups // 2
    hot = tok_rows // 4
    dpart = depth // n
    bs = min(dpart, 512)
    nb = dpart // bs
    all_rows = experts * hot
    vmem = pl.BlockSpec(memory_space=pltpu.VMEM)
    hbm = pl.BlockSpec(memory_space=pl.ANY)
    dma = pltpu.SemaphoreType.DMA
    chunk = (experts, hot, depth)
    buffers = [
        pltpu.VMEM((2,) + chunk, bf16),
        pltpu.VMEM((2, 2) + chunk, bf16),
        pltpu.VMEM((depth, 2 * ff), bf16),
        pltpu.VMEM((ff, depth), bf16),
        pltpu.VMEM(chunk, f32),
        pltpu.VMEM(chunk, bf16),
        pltpu.VMEM(chunk, bf16),
        pltpu.VMEM(chunk, bf16),
        pltpu.VMEM(chunk, bf16),
        pltpu.VMEM((2 * all_rows, 2 * ff), bf16),
        pltpu.VMEM((2 * all_rows, ff), bf16),
        pltpu.VMEM((n * nb, bs, 2 * ff), f32),
        pltpu.VMEM((n * nb, ff, bs), f32),
        pltpu.VMEM((n - 1, nb, bs, 2 * ff), f32),
        pltpu.VMEM((n - 1, nb, ff, bs), f32),
        pltpu.VMEM((all_rows, tok_rows), bf16),
    ]
    held = sum(math.prod(b.shape) * b.dtype.itemsize for b in buffers)
    moved = 3 * tok_rows * depth * 2 + 3 * dpart * ff * 4
    return pl.pallas_call(
        functools.partial(kernel, n, experts, hot, bs),
        out_shape=(
            jax.ShapeDtypeStruct((tok_rows, depth), bf16),
            jax.ShapeDtypeStruct((dpart, ff), f32),
            jax.ShapeDtypeStruct((dpart, ff), f32),
            jax.ShapeDtypeStruct((ff, dpart), f32),
        ),
        in_specs=[vmem] * 4 + [hbm] * 3,
        out_specs=(vmem,) * 4,
        scratch_shapes=buffers + [
            dma((3,)),
            dma((n - 1, 3)),
            dma((n - 1, 3)),
            dma((2, experts)),
            dma((2, experts)),
            dma((2, experts)),
            dma((2, experts)),
            dma((experts,)),
            dma((experts,)),
            dma((experts,)),
            dma((experts,)),
            dma((n - 1, 2)),
            dma((n - 1, 2)),
        ],
        compiler_params=pltpu.CompilerParams(
            collective_id=0, has_side_effects=True, vmem_limit_bytes=held + moved + spare_bytes
        ),
        name="expert_layer",
    )(tokens, out_grad, expert_ids, gate_fixed, w_gate, w_up, w_down)


def per_device(
    tokens,
    out_grad,
    expert_ids,
    gate_fixed,
    w_gate,
    w_up,
    w_down,
    m_gate,
    m_up,
    m_down,
    v_gate,
    v_up,
    v_down,
):
    n = lax.axis_size("dp")
    groups = lax.axis_size("expert")
    input_grad, gate_grad, up_grad, down_grad = expert_layer(
        n, groups, tokens, out_grad, expert_ids.reshape(1, -1), gate_fixed.reshape(1, -1), w_gate, w_up, w_down
    )
    gate_new, gate_first, gate_second = adam_update(w_gate[0], gate_grad, m_gate[0], v_gate[0])
    up_new, up_first, up_second = adam_update(w_up[0], up_grad, m_up[0], v_up[0])
    down_new, down_first, down_second = adam_update(w_down[0], down_grad, m_down[0], v_down[0])
    return (
        input_grad,
        gate_new[None],
        up_new[None],
        down_new[None],
        gate_first[None],
        up_first[None],
        down_first[None],
        gate_second[None],
        up_second[None],
        down_second[None],
    )


def solution(mesh):
    return jax.shard_map(
        per_device,
        mesh=mesh,
        in_specs=(
            P(("dp", "expert"), None),
            P(("dp", "expert"), None),
            P(("dp", "expert"), None),
            P(("dp", "expert"), None),
            P("expert", "dp", None),
            P("expert", "dp", None),
            P("expert", None, "dp"),
            P("expert", "dp", None),
            P("expert", "dp", None),
            P("expert", None, "dp"),
            P("expert", "dp", None),
            P("expert", "dp", None),
            P("expert", None, "dp"),
        ),
        out_specs=(
            P(("dp", "expert"), None),
            P("expert", "dp", None),
            P("expert", "dp", None),
            P("expert", None, "dp"),
            P("expert", "dp", None),
            P("expert", "dp", None),
            P("expert", None, "dp"),
            P("expert", "dp", None),
            P("expert", "dp", None),
            P("expert", None, "dp"),
        ),
        check_vma=False,
    )
```

```python
import functools

import jax
import jax.numpy as jnp
from jax import lax
from jax.experimental import pallas as pl
from jax.experimental.pallas import tpu as pltpu
from jax.sharding import PartitionSpec as P

beta_one = 0.9
beta_two = 0.95
learn_rate = 0.002
decay_rate = 0.1
epsilon = 1e-08
bias_one = 1.0 - beta_one**20
bias_two = 1.0 - beta_two**20
fixed_scale = 1.0 / 65536.0

f32 = jnp.float32
bf16 = jnp.bfloat16
MESH = pl.DeviceIdType.MESH
lhs_t = (((0,), (0,)), ((), ()))
rhs_t = (((1,), (1,)), ((), ()))


def adam_update(weight, gradient, moment_one, moment_two):
    weight_full = weight.astype(f32)
    first_new = beta_one * moment_one + (1.0 - beta_one) * gradient
    second_new = beta_two * moment_two + (1.0 - beta_two) * gradient * gradient
    update = (
        first_new * (1.0 / bias_one) / (jnp.sqrt(second_new * (1.0 / bias_two)) + epsilon)
        + decay_rate * weight_full
    )
    return ((weight_full - learn_rate * update).astype(bf16), first_new, second_new)


def flipped(index, mask, count):
    total, bit = 0, 1
    while bit < count:
        here = lax.rem(lax.div(index, bit), 2)
        total = total + (1 - here if mask & bit else here) * bit
        bit *= 2
    return total


def remote(src, dst, send, recv, where):
    return pltpu.make_async_remote_copy(
        src_ref=src, dst_ref=dst, send_sem=send, recv_sem=recv, device_id=where, device_id_type=MESH
    )


def kernel(
    n, experts, hot, bs,
    tok_ref, og_ref, ids_ref, fix_ref, wg_ref, wu_ref, wd_ref,
    grad_ref, gate_out, up_out, down_out,
    slots, rows, gu, dn, part, psend, precv, rsend, ret, inner, hid, gu_grad, dn_grad,
    gu_recv, dn_recv, pick,
    wl, ws, wr, d_send, d_recv, f_send, f_recv, p_send, p_recv, r_send, r_recv, g_send, g_recv,
):
    tok_rows, depth = tok_ref.shape
    ff = wg_ref.shape[2]
    dpart = depth // n
    nb = dpart // bs
    all_rows = experts * hot
    d = lax.axis_index("dp")
    g = lax.axis_index("expert")
    e = lax.div(g, 2)
    s = lax.rem(g, 2)
    partner = g + 1 - 2 * s
    half = experts // 2
    quarter = experts // 4
    near, far = list(range(half)), list(range(half, experts))
    order = near[:quarter] + far[:quarter] + near[quarter:] + far[quarter:]
    place = {k: pos for pos, k in enumerate(order)}
    arrivals = near[1:3] + far[:2] + near[3:] + far[2:]
    window = 3

    def peer(k):
        return {"expert": 2 * flipped(e, k, experts) + s}

    def dp_at(k):
        return lax.rem(d + k, n)

    def places(owner):
        at = pl.ds(pl.multiple_of(owner * dpart, dpart), dpart)
        return [gu.at[at, pl.ds(0, ff)], gu.at[at, pl.ds(ff, ff)], dn.at[:, at]]

    weights = [wg_ref.at[0], wu_ref.at[0], wd_ref.at[0]]
    local = [pltpu.make_async_copy(w, to, wl.at[i]) for i, (w, to) in enumerate(zip(weights, places(d)))]
    for copy in local:
        copy.start()

    barrier = pltpu.get_barrier_semaphore()
    for k in range(1, experts):
        pl.semaphore_signal(barrier, inc=1, device_id=peer(k), device_id_type=MESH)
    pl.semaphore_signal(barrier, inc=1, device_id={"expert": partner}, device_id_type=MESH)
    for k in range(1, n):
        pl.semaphore_signal(barrier, inc=1, device_id={"dp": dp_at(k)}, device_id_type=MESH)

    ids = ids_ref[...]
    onehot = (ids == lax.broadcasted_iota(jnp.int32, (experts, tok_rows), 0)).astype(f32)
    row_at = lax.broadcasted_iota(jnp.int32, (tok_rows, tok_rows), 0)
    col_at = lax.broadcasted_iota(jnp.int32, (tok_rows, tok_rows), 1)
    before = jnp.where(row_at < col_at, 1.0, 0.0).astype(bf16)
    counts = jnp.dot(onehot.astype(bf16), before, preferred_element_type=f32)
    position = jnp.sum(counts * onehot, axis=0, keepdims=True)
    slot = ids.astype(f32) * hot + position
    heights = lax.broadcasted_iota(jnp.int32, (all_rows, tok_rows), 0).astype(f32)
    pick[...] = jnp.where(slot == heights, 1.0, 0.0).astype(bf16)
    scale_row = fix_ref[...].astype(f32) * fixed_scale
    scale = jnp.sum(jnp.where(row_at == col_at, scale_row, 0.0), axis=1, keepdims=True)
    cot = (og_ref[...].astype(f32) * scale).astype(bf16)
    for a, source in ((0, tok_ref[...]), (1, cot)):
        moved = jnp.dot(pick[...], source, preferred_element_type=f32)
        slots[a] = moved.astype(bf16).reshape(experts, hot, depth)

    pl.semaphore_wait(barrier, experts + n - 1)

    sends = []

    def go(copy):
        copy.start()
        sends.append(copy)

    def forward(a, pos):
        go(remote(rows.at[a, 0, pos], rows.at[a, 1, pos], f_send.at[a, pos], f_recv.at[a, pos],
                  {"expert": partner}))

    def direct(a, pos):
        k = order[pos]
        go(remote(slots.at[a, flipped(e, k, experts)], rows.at[a, 0, pos], d_send.at[a, pos],
                  d_recv.at[a, pos], peer(k)))

    waiting = [(a, place[k]) for k in far for a in range(2)]
    for a, pos in waiting[:window]:
        direct(a, pos)
    for k in near[1:]:
        for a in range(2):
            direct(a, place[k])
    for a in range(2):
        rows[a, 0, 0] = slots[a, e]
        forward(a, 0)
    for k in range(1, n):
        for i in range(3):
            go(remote(weights[i], places(d)[i], ws.at[k - 1, i], wr.at[k - 1, i], {"dp": dp_at(k)}))

    started = window
    for k in arrivals:
        pos = place[k]
        for a in range(2):
            remote(rows.at[a, 0, pos], rows.at[a, 0, pos], d_send.at[a, pos], d_recv.at[a, pos],
                   peer(k)).wait_recv()
            if k >= half and started < len(waiting):
                direct(*waiting[started])
                started += 1
            forward(a, pos)

    for copy in local:
        copy.wait()
    for k in range(1, n):
        arriving = places(lax.rem(d + n - k, n))
        for i in range(3):
            remote(arriving[i], arriving[i], ws.at[k - 1, i], wr.at[k - 1, i], {"dp": dp_at(k)}).wait_recv()

    def through(b, lo, many):
        here = pl.ds(lo, many)
        x = rows[0, b, here].reshape(many * hot, depth)
        c = rows[1, b, here].reshape(many * hot, depth)
        pre = jnp.dot(x, gu[...], preferred_element_type=f32)
        hidden_cot = lax.dot_general(c, dn[...], rhs_t, preferred_element_type=f32)
        gate_pre, up_pre = pre[:, :ff], pre[:, ff:]
        sig = jax.nn.sigmoid(gate_pre)
        active = gate_pre * sig
        at = pl.ds(b * all_rows + lo * hot, many * hot)
        hid[at] = (active * up_pre).astype(bf16)
        inner[at, pl.ds(ff, ff)] = (hidden_cot * active).astype(bf16)
        inner[at, pl.ds(0, ff)] = (hidden_cot * up_pre * sig * (1.0 + gate_pre * (1.0 - sig))).astype(bf16)
        return lax.dot_general(inner[at], gu[...], rhs_t, preferred_element_type=f32).reshape(many, hot, depth)

    def forwarded(lo):
        for pos in range(lo, lo + half):
            for a in range(2):
                remote(rows.at[a, 1, pos], rows.at[a, 1, pos], f_send.at[a, pos], f_recv.at[a, pos],
                       {"expert": partner}).wait_recv()
        psend[pl.ds(lo, half)] = through(1, lo, half).astype(bf16)
        for pos in list(range(lo + quarter, lo + half)) + list(range(lo, lo + quarter)):
            go(remote(psend.at[pos], precv.at[pos], p_send.at[pos], p_recv.at[pos], {"expert": partner}))

    def weight_block(i):
        block = lax.rem((d + 1) * nb + i, n * nb)
        at = pl.ds(pl.multiple_of(block * bs, bs), bs)
        x = rows[0, :, :, :, at].reshape(2 * all_rows, bs)
        c = rows[1, :, :, :, at].reshape(2 * all_rows, bs)
        gu_grad[block] = lax.dot_general(x, inner[...], lhs_t, preferred_element_type=f32)
        dn_grad[block] = lax.dot_general(hid[...], c, lhs_t, preferred_element_type=f32)
        if i % nb == nb - 1 and i < (n - 1) * nb:
            k = i // nb + 1
            theirs = pl.ds(dp_at(k) * nb, nb)
            go(remote(gu_grad.at[theirs], gu_recv.at[k - 1], g_send.at[k - 1, 0], g_recv.at[k - 1, 0],
                      {"dp": dp_at(k)}))
            go(remote(dn_grad.at[theirs], dn_recv.at[k - 1], g_send.at[k - 1, 1], g_recv.at[k - 1, 1],
                      {"dp": dp_at(k)}))

    def give_back(pos):
        k = order[pos]
        remote(precv.at[pos], precv.at[pos], p_send.at[pos], p_recv.at[pos], {"expert": partner}).wait_recv()
        total = (part[pos] + precv[pos].astype(f32)).astype(bf16)
        if k == 0:
            ret[e] = total
        else:
            rsend[pos] = total
            go(remote(rsend.at[pos], ret.at[e], r_send.at[pos], r_recv.at[pos], peer(k)))

    blocks = list(range(n * nb))
    forwarded(0)
    part[...] = through(0, 0, experts)
    for k in far[:quarter]:
        give_back(place[k])
    forwarded(half)
    for k in near[1:quarter] + near[:1] + far[quarter:] + near[quarter:]:
        give_back(place[k])
        if blocks and k:
            weight_block(blocks.pop(0))
    for i in blocks:
        weight_block(i)

    for k in range(1, n):
        remote(gu_recv.at[k - 1], gu_recv.at[k - 1], g_send.at[k - 1, 0], g_recv.at[k - 1, 0],
               {"dp": dp_at(k)}).wait_recv()
        remote(dn_recv.at[k - 1], dn_recv.at[k - 1], g_send.at[k - 1, 1], g_recv.at[k - 1, 1],
               {"dp": dp_at(k)}).wait_recv()
    for i in range(nb):
        at = pl.ds(i * bs, bs)
        both = gu_grad[d * nb + i]
        down = dn_grad[d * nb + i]
        for k in range(1, n):
            both = both + gu_recv[k - 1, i]
            down = down + dn_recv[k - 1, i]
        gate_out[at] = both[:, :ff]
        up_out[at] = both[:, ff:]
        down_out[:, at] = down

    for pos, k in enumerate(order):
        if k:
            at = ret.at[flipped(e, k, experts)]
            remote(at, at, r_send.at[pos], r_recv.at[pos], peer(k)).wait_recv()
    back = ret[...].reshape(all_rows, depth)
    grad_ref[...] = lax.dot_general(pick[...], back, lhs_t, preferred_element_type=f32).astype(bf16)
    for copy in sends:
        copy.wait_send()


def expert_layer(n, groups, tokens, out_grad, expert_ids, gate_fixed, w_gate, w_up, w_down):
    tok_rows, depth = tokens.shape
    ff = w_gate.shape[2]
    experts = groups // 2
    hot = tok_rows // 4
    dpart = depth // n
    bs = min(dpart, 512)
    nb = dpart // bs
    all_rows = experts * hot
    vmem = pl.BlockSpec(memory_space=pltpu.VMEM)
    hbm = pl.BlockSpec(memory_space=pl.ANY)
    dma = pltpu.SemaphoreType.DMA
    chunk = (experts, hot, depth)
    buffers = [
        pltpu.VMEM((2,) + chunk, bf16),
        pltpu.VMEM((2, 2) + chunk, bf16),
        pltpu.VMEM((depth, 2 * ff), bf16),
        pltpu.VMEM((ff, depth), bf16),
        pltpu.VMEM(chunk, f32),
        pltpu.VMEM(chunk, bf16),
        pltpu.VMEM(chunk, bf16),
        pltpu.VMEM(chunk, bf16),
        pltpu.VMEM(chunk, bf16),
        pltpu.VMEM((2 * all_rows, 2 * ff), bf16),
        pltpu.VMEM((2 * all_rows, ff), bf16),
        pltpu.VMEM((n * nb, bs, 2 * ff), f32),
        pltpu.VMEM((n * nb, ff, bs), f32),
        pltpu.VMEM((n - 1, nb, bs, 2 * ff), f32),
        pltpu.VMEM((n - 1, nb, ff, bs), f32),
        pltpu.VMEM((all_rows, tok_rows), bf16),
    ]
    return pl.pallas_call(
        functools.partial(kernel, n, experts, hot, bs),
        out_shape=(
            jax.ShapeDtypeStruct((tok_rows, depth), bf16),
            jax.ShapeDtypeStruct((dpart, ff), f32),
            jax.ShapeDtypeStruct((dpart, ff), f32),
            jax.ShapeDtypeStruct((ff, dpart), f32),
        ),
        in_specs=[vmem] * 4 + [hbm] * 3,
        out_specs=(vmem,) * 4,
        scratch_shapes=buffers + [
            dma((3,)),
            dma((n - 1, 3)),
            dma((n - 1, 3)),
            dma((2, experts)),
            dma((2, experts)),
            dma((2, experts)),
            dma((2, experts)),
            dma((experts,)),
            dma((experts,)),
            dma((experts,)),
            dma((experts,)),
            dma((n - 1, 2)),
            dma((n - 1, 2)),
        ],
        compiler_params=pltpu.CompilerParams(
            collective_id=0, has_side_effects=True, vmem_limit_bytes=60 * 1024 * 1024
        ),
        name="expert_layer",
    )(tokens, out_grad, expert_ids, gate_fixed, w_gate, w_up, w_down)


def per_device(
    tokens,
    out_grad,
    expert_ids,
    gate_fixed,
    w_gate,
    w_up,
    w_down,
    m_gate,
    m_up,
    m_down,
    v_gate,
    v_up,
    v_down,
):
    n = lax.axis_size("dp")
    groups = lax.axis_size("expert")
    input_grad, gate_grad, up_grad, down_grad = expert_layer(
        n, groups, tokens, out_grad, expert_ids.reshape(1, -1), gate_fixed.reshape(1, -1), w_gate, w_up, w_down
    )
    gate_new, gate_first, gate_second = adam_update(w_gate[0], gate_grad, m_gate[0], v_gate[0])
    up_new, up_first, up_second = adam_update(w_up[0], up_grad, m_up[0], v_up[0])
    down_new, down_first, down_second = adam_update(w_down[0], down_grad, m_down[0], v_down[0])
    return (
        input_grad,
        gate_new[None],
        up_new[None],
        down_new[None],
        gate_first[None],
        up_first[None],
        down_first[None],
        gate_second[None],
        up_second[None],
        down_second[None],
    )


def solution(mesh):
    return jax.shard_map(
        per_device,
        mesh=mesh,
        in_specs=(
            P(("dp", "expert"), None),
            P(("dp", "expert"), None),
            P(("dp", "expert"), None),
            P(("dp", "expert"), None),
            P("expert", "dp", None),
            P("expert", "dp", None),
            P("expert", None, "dp"),
            P("expert", "dp", None),
            P("expert", "dp", None),
            P("expert", None, "dp"),
            P("expert", "dp", None),
            P("expert", "dp", None),
            P("expert", None, "dp"),
        ),
        out_specs=(
            P(("dp", "expert"), None),
            P("expert", "dp", None),
            P("expert", "dp", None),
            P("expert", None, "dp"),
            P("expert", "dp", None),
            P("expert", "dp", None),
            P("expert", None, "dp"),
            P("expert", "dp", None),
            P("expert", "dp", None),
            P("expert", None, "dp"),
        ),
        check_vma=False,
    )
```

```python
import functools

import jax
import jax.numpy as jnp
from jax import lax
from jax.experimental import pallas as pl
from jax.experimental.pallas import tpu as pltpu
from jax.sharding import PartitionSpec as P

beta_one = 0.9
beta_two = 0.95
learn_rate = 0.002
decay_rate = 0.1
epsilon = 1e-08
bias_one = 1.0 - beta_one**20
bias_two = 1.0 - beta_two**20
fixed_scale = 1.0 / 65536.0

f32 = jnp.float32
bf16 = jnp.bfloat16
MESH = pl.DeviceIdType.MESH
lhs_t = (((0,), (0,)), ((), ()))
rhs_t = (((1,), (1,)), ((), ()))


def adam_update(weight, gradient, moment_one, moment_two):
    weight_full = weight.astype(f32)
    first_new = beta_one * moment_one + (1.0 - beta_one) * gradient
    second_new = beta_two * moment_two + (1.0 - beta_two) * gradient * gradient
    update = (
        first_new * (1.0 / bias_one) / (jnp.sqrt(second_new * (1.0 / bias_two)) + epsilon)
        + decay_rate * weight_full
    )
    return ((weight_full - learn_rate * update).astype(bf16), first_new, second_new)


def flipped(index, mask, count):
    total, bit = 0, 1
    while bit < count:
        here = lax.rem(lax.div(index, bit), 2)
        total = total + (1 - here if mask & bit else here) * bit
        bit *= 2
    return total


def remote(src, dst, send, recv, where):
    return pltpu.make_async_remote_copy(
        src_ref=src, dst_ref=dst, send_sem=send, recv_sem=recv, device_id=where, device_id_type=MESH
    )


def kernel(
    n, experts, hot, bs,
    tok_ref, og_ref, ids_ref, fix_ref, wg_ref, wu_ref, wd_ref,
    grad_ref, gate_out, up_out, down_out,
    slots, rows, gu, dn, part, psend, precv, rsend, ret, inner, hid, gu_grad, dn_grad,
    gu_recv, dn_recv, pick,
    wl, ws, wr, d_send, d_recv, f_send, f_recv, p_send, p_recv, r_send, r_recv, g_send, g_recv,
):
    tok_rows, depth = tok_ref.shape
    ff = wg_ref.shape[2]
    dpart = depth // n
    nb = dpart // bs
    all_rows = experts * hot
    d = lax.axis_index("dp")
    g = lax.axis_index("expert")
    e = lax.div(g, 2)
    s = lax.rem(g, 2)
    partner = g + 1 - 2 * s
    half = experts // 2
    quarter = experts // 4
    near, far = list(range(half)), list(range(half, experts))
    order = near[:quarter] + far[:quarter] + near[quarter:] + far[quarter:]
    place = {k: pos for pos, k in enumerate(order)}
    arrivals = near[1:quarter + 1] + far[:quarter] + near[quarter + 1:] + far[quarter:]
    window = 3

    def peer(k):
        return {"expert": 2 * flipped(e, k, experts) + s}

    def dp_at(k):
        return lax.rem(d + k, n)

    def places(owner):
        at = pl.ds(pl.multiple_of(owner * dpart, dpart), dpart)
        return [gu.at[at, pl.ds(0, ff)], gu.at[at, pl.ds(ff, ff)], dn.at[:, at]]

    weights = [wg_ref.at[0], wu_ref.at[0], wd_ref.at[0]]
    local = [pltpu.make_async_copy(w, to, wl.at[i]) for i, (w, to) in enumerate(zip(weights, places(d)))]
    for copy in local:
        copy.start()

    barrier = pltpu.get_barrier_semaphore()
    for k in range(1, experts):
        pl.semaphore_signal(barrier, inc=1, device_id=peer(k), device_id_type=MESH)
    pl.semaphore_signal(barrier, inc=1, device_id={"expert": partner}, device_id_type=MESH)
    for k in range(1, n):
        pl.semaphore_signal(barrier, inc=1, device_id={"dp": dp_at(k)}, device_id_type=MESH)

    ids = ids_ref[...]
    onehot = (ids == lax.broadcasted_iota(jnp.int32, (experts, tok_rows), 0)).astype(f32)
    row_at = lax.broadcasted_iota(jnp.int32, (tok_rows, tok_rows), 0)
    col_at = lax.broadcasted_iota(jnp.int32, (tok_rows, tok_rows), 1)
    before = jnp.where(row_at < col_at, 1.0, 0.0).astype(bf16)
    counts = jnp.dot(onehot.astype(bf16), before, preferred_element_type=f32)
    position = jnp.sum(counts * onehot, axis=0, keepdims=True)
    slot = ids.astype(f32) * hot + position
    heights = lax.broadcasted_iota(jnp.int32, (all_rows, tok_rows), 0).astype(f32)
    pick[...] = jnp.where(slot == heights, 1.0, 0.0).astype(bf16)
    scale_row = fix_ref[...].astype(f32) * fixed_scale
    scale = jnp.sum(jnp.where(row_at == col_at, scale_row, 0.0), axis=1, keepdims=True)
    cot = (og_ref[...].astype(f32) * scale).astype(bf16)
    for a, source in ((0, tok_ref[...]), (1, cot)):
        moved = jnp.dot(pick[...], source, preferred_element_type=f32)
        slots[a] = moved.astype(bf16).reshape(experts, hot, depth)

    pl.semaphore_wait(barrier, experts + n - 1)

    sends = []

    def go(copy):
        copy.start()
        sends.append(copy)

    def forward(a, pos):
        go(remote(rows.at[a, 0, pos], rows.at[a, 1, pos], f_send.at[a, pos], f_recv.at[a, pos],
                  {"expert": partner}))

    def direct(a, pos):
        k = order[pos]
        go(remote(slots.at[a, flipped(e, k, experts)], rows.at[a, 0, pos], d_send.at[a, pos],
                  d_recv.at[a, pos], peer(k)))

    waiting = [(a, place[k]) for k in far for a in range(2)]
    for a, pos in waiting[:window]:
        direct(a, pos)
    for k in near[1:]:
        for a in range(2):
            direct(a, place[k])
    for a in range(2):
        rows[a, 0, 0] = slots[a, e]
        forward(a, 0)
    for k in range(1, n):
        for i in range(3):
            go(remote(weights[i], places(d)[i], ws.at[k - 1, i], wr.at[k - 1, i], {"dp": dp_at(k)}))

    def weights_here():
        for copy in local:
            copy.wait()
        for k in range(1, n):
            arriving = places(lax.rem(d + n - k, n))
            for i in range(3):
                remote(arriving[i], arriving[i], ws.at[k - 1, i], wr.at[k - 1, i], {"dp": dp_at(k)}).wait_recv()

    def through(b, lo, many):
        here = pl.ds(lo, many)
        x = rows[0, b, here].reshape(many * hot, depth)
        c = rows[1, b, here].reshape(many * hot, depth)
        pre = jnp.dot(x, gu[...], preferred_element_type=f32)
        hidden_cot = lax.dot_general(c, dn[...], rhs_t, preferred_element_type=f32)
        gate_pre, up_pre = pre[:, :ff], pre[:, ff:]
        sig = jax.nn.sigmoid(gate_pre)
        active = gate_pre * sig
        at = pl.ds(b * all_rows + lo * hot, many * hot)
        hid[at] = (active * up_pre).astype(bf16)
        inner[at, pl.ds(ff, ff)] = (hidden_cot * active).astype(bf16)
        inner[at, pl.ds(0, ff)] = (hidden_cot * up_pre * sig * (1.0 + gate_pre * (1.0 - sig))).astype(bf16)
        return lax.dot_general(inner[at], gu[...], rhs_t, preferred_element_type=f32).reshape(many, hot, depth)

    def forwarded(lo):
        for pos in range(lo, lo + half):
            for a in range(2):
                remote(rows.at[a, 1, pos], rows.at[a, 1, pos], f_send.at[a, pos], f_recv.at[a, pos],
                       {"expert": partner}).wait_recv()
        psend[pl.ds(lo, half)] = through(1, lo, half).astype(bf16)

    def share(lo):
        for pos in list(range(lo + quarter, lo + half)) + list(range(lo, lo + quarter)):
            go(remote(psend.at[pos], precv.at[pos], p_send.at[pos], p_recv.at[pos], {"expert": partner}))

    started = window
    for k in arrivals:
        pos = place[k]
        for a in range(2):
            remote(rows.at[a, 0, pos], rows.at[a, 0, pos], d_send.at[a, pos], d_recv.at[a, pos],
                   peer(k)).wait_recv()
            if k >= half and started < len(waiting):
                direct(*waiting[started])
                started += 1
            forward(a, pos)
        if k == half - 1:
            weights_here()
            part[pl.ds(0, half)] = through(0, 0, half)
        if k == experts - 2:
            forwarded(0)

    def weight_block(i):
        block = lax.rem((d + 1) * nb + i, n * nb)
        at = pl.ds(pl.multiple_of(block * bs, bs), bs)
        x = rows[0, :, :, :, at].reshape(2 * all_rows, bs)
        c = rows[1, :, :, :, at].reshape(2 * all_rows, bs)
        gu_grad[block] = lax.dot_general(x, inner[...], lhs_t, preferred_element_type=f32)
        dn_grad[block] = lax.dot_general(hid[...], c, lhs_t, preferred_element_type=f32)
        if i % nb == nb - 1 and i < (n - 1) * nb:
            k = i // nb + 1
            theirs = pl.ds(dp_at(k) * nb, nb)
            go(remote(gu_grad.at[theirs], gu_recv.at[k - 1], g_send.at[k - 1, 0], g_recv.at[k - 1, 0],
                      {"dp": dp_at(k)}))
            go(remote(dn_grad.at[theirs], dn_recv.at[k - 1], g_send.at[k - 1, 1], g_recv.at[k - 1, 1],
                      {"dp": dp_at(k)}))

    def give_back(pos):
        k = order[pos]
        remote(precv.at[pos], precv.at[pos], p_send.at[pos], p_recv.at[pos], {"expert": partner}).wait_recv()
        total = (part[pos] + precv[pos].astype(f32)).astype(bf16)
        if k == 0:
            ret[e] = total
        else:
            rsend[pos] = total
            go(remote(rsend.at[pos], ret.at[e], r_send.at[pos], r_recv.at[pos], peer(k)))

    blocks = list(range(n * nb))
    share(0)
    part[pl.ds(half, half)] = through(0, half, half)
    for k in far[:quarter]:
        give_back(place[k])
    forwarded(half)
    share(half)
    for k in near[1:quarter] + near[:1] + far[quarter:] + near[quarter:]:
        give_back(place[k])
        if blocks and k:
            weight_block(blocks.pop(0))
    for i in blocks:
        weight_block(i)

    for k in range(1, n):
        remote(gu_recv.at[k - 1], gu_recv.at[k - 1], g_send.at[k - 1, 0], g_recv.at[k - 1, 0],
               {"dp": dp_at(k)}).wait_recv()
        remote(dn_recv.at[k - 1], dn_recv.at[k - 1], g_send.at[k - 1, 1], g_recv.at[k - 1, 1],
               {"dp": dp_at(k)}).wait_recv()
    for i in range(nb):
        at = pl.ds(i * bs, bs)
        both = gu_grad[d * nb + i]
        down = dn_grad[d * nb + i]
        for k in range(1, n):
            both = both + gu_recv[k - 1, i]
            down = down + dn_recv[k - 1, i]
        gate_out[at] = both[:, :ff]
        up_out[at] = both[:, ff:]
        down_out[:, at] = down

    for pos, k in enumerate(order):
        if k:
            at = ret.at[flipped(e, k, experts)]
            remote(at, at, r_send.at[pos], r_recv.at[pos], peer(k)).wait_recv()
    back = ret[...].reshape(all_rows, depth)
    grad_ref[...] = lax.dot_general(pick[...], back, lhs_t, preferred_element_type=f32).astype(bf16)
    for copy in sends:
        copy.wait_send()


def expert_layer(n, groups, tokens, out_grad, expert_ids, gate_fixed, w_gate, w_up, w_down):
    tok_rows, depth = tokens.shape
    ff = w_gate.shape[2]
    experts = groups // 2
    hot = tok_rows // 4
    dpart = depth // n
    bs = min(dpart, 512)
    nb = dpart // bs
    all_rows = experts * hot
    vmem = pl.BlockSpec(memory_space=pltpu.VMEM)
    hbm = pl.BlockSpec(memory_space=pl.ANY)
    dma = pltpu.SemaphoreType.DMA
    chunk = (experts, hot, depth)
    buffers = [
        pltpu.VMEM((2,) + chunk, bf16),
        pltpu.VMEM((2, 2) + chunk, bf16),
        pltpu.VMEM((depth, 2 * ff), bf16),
        pltpu.VMEM((ff, depth), bf16),
        pltpu.VMEM(chunk, f32),
        pltpu.VMEM(chunk, bf16),
        pltpu.VMEM(chunk, bf16),
        pltpu.VMEM(chunk, bf16),
        pltpu.VMEM(chunk, bf16),
        pltpu.VMEM((2 * all_rows, 2 * ff), bf16),
        pltpu.VMEM((2 * all_rows, ff), bf16),
        pltpu.VMEM((n * nb, bs, 2 * ff), f32),
        pltpu.VMEM((n * nb, ff, bs), f32),
        pltpu.VMEM((n - 1, nb, bs, 2 * ff), f32),
        pltpu.VMEM((n - 1, nb, ff, bs), f32),
        pltpu.VMEM((all_rows, tok_rows), bf16),
    ]
    return pl.pallas_call(
        functools.partial(kernel, n, experts, hot, bs),
        out_shape=(
            jax.ShapeDtypeStruct((tok_rows, depth), bf16),
            jax.ShapeDtypeStruct((dpart, ff), f32),
            jax.ShapeDtypeStruct((dpart, ff), f32),
            jax.ShapeDtypeStruct((ff, dpart), f32),
        ),
        in_specs=[vmem] * 4 + [hbm] * 3,
        out_specs=(vmem,) * 4,
        scratch_shapes=buffers + [
            dma((3,)),
            dma((n - 1, 3)),
            dma((n - 1, 3)),
            dma((2, experts)),
            dma((2, experts)),
            dma((2, experts)),
            dma((2, experts)),
            dma((experts,)),
            dma((experts,)),
            dma((experts,)),
            dma((experts,)),
            dma((n - 1, 2)),
            dma((n - 1, 2)),
        ],
        compiler_params=pltpu.CompilerParams(
            collective_id=0, has_side_effects=True, vmem_limit_bytes=60 * 1024 * 1024
        ),
        name="expert_layer",
    )(tokens, out_grad, expert_ids, gate_fixed, w_gate, w_up, w_down)


def per_device(
    tokens,
    out_grad,
    expert_ids,
    gate_fixed,
    w_gate,
    w_up,
    w_down,
    m_gate,
    m_up,
    m_down,
    v_gate,
    v_up,
    v_down,
):
    n = lax.axis_size("dp")
    groups = lax.axis_size("expert")
    input_grad, gate_grad, up_grad, down_grad = expert_layer(
        n, groups, tokens, out_grad, expert_ids.reshape(1, -1), gate_fixed.reshape(1, -1), w_gate, w_up, w_down
    )
    gate_new, gate_first, gate_second = adam_update(w_gate[0], gate_grad, m_gate[0], v_gate[0])
    up_new, up_first, up_second = adam_update(w_up[0], up_grad, m_up[0], v_up[0])
    down_new, down_first, down_second = adam_update(w_down[0], down_grad, m_down[0], v_down[0])
    return (
        input_grad,
        gate_new[None],
        up_new[None],
        down_new[None],
        gate_first[None],
        up_first[None],
        down_first[None],
        gate_second[None],
        up_second[None],
        down_second[None],
    )


def solution(mesh):
    return jax.shard_map(
        per_device,
        mesh=mesh,
        in_specs=(
            P(("dp", "expert"), None),
            P(("dp", "expert"), None),
            P(("dp", "expert"), None),
            P(("dp", "expert"), None),
            P("expert", "dp", None),
            P("expert", "dp", None),
            P("expert", None, "dp"),
            P("expert", "dp", None),
            P("expert", "dp", None),
            P("expert", None, "dp"),
            P("expert", "dp", None),
            P("expert", "dp", None),
            P("expert", None, "dp"),
        ),
        out_specs=(
            P(("dp", "expert"), None),
            P("expert", "dp", None),
            P("expert", "dp", None),
            P("expert", None, "dp"),
            P("expert", "dp", None),
            P("expert", "dp", None),
            P("expert", None, "dp"),
            P("expert", "dp", None),
            P("expert", "dp", None),
            P("expert", None, "dp"),
        ),
        check_vma=False,
    )
```
